32 devices in a mesh: rows: 4 (over z), protos: 8 (over y, x, core).
Axes of the slice: x: 2, y: 2, z: 4, core: 2. Of those that a mesh axis runs over, the one named last changes fastest.
Arguments:
- teacher_rows: bfloat16 [4096, 256], P(('rows', 'protos')), may hold values from -16 to 16
- student_rows: bfloat16 [4096, 256], P(('rows', 'protos')), may hold values from -16 to 16
- prototypes: bfloat16 [256, 131072], P(None, 'protos'), may hold values from -16 to 16
Outputs:
- row_grads: float32 [4096, 256], P(('rows', 'protos'))
- row_loss: float32 [4096], P(('rows', 'protos'))
The draws below stay inside these ranges and needn't reach their ends.
All inputs are finite; a program needn't handle non-finite values.
Results may differ from the reference program's by a relative error of at most 0.0015.
Values may be sent and summed in bfloat16 or wider, within the bound.
No kernel may reach another device: no remote copies, remote signals or barrier semaphores. Data moves between devices by JAX's collectives and lax.ppermute only.
A program may use at most 192 MiB of HBM per device.

```python
import jax
import jax.numpy as jnp
from jax import lax

BOTTLE = 256
PROTOTYPES = 131072
ITERS = 3
BATCH = 4096


def center_table(key):
    return jax.random.truncated_normal(jax.random.fold_in(key, 101), -4.0, 4.0, (16, BOTTLE), jnp.float32)


def crop_labels(key):
    cuts = jax.random.randint(jax.random.fold_in(key, 102), (15,), 0, BATCH)
    positions = jnp.arange(BATCH, dtype=jnp.int32)
    segment = jnp.sum((positions[:, None] >= cuts[None, :]).astype(jnp.int32), axis=1)
    order = jax.random.permutation(jax.random.fold_in(key, 110), 16)
    return order[segment]


def crop_mixture(key):
    centers = center_table(key)
    labels = crop_labels(key)
    following = (labels + 1) % 16
    return centers[labels] + centers[following]


def draw_teacher_rows(key, part):
    mixture = crop_mixture(key)
    noise = jax.random.truncated_normal(jax.random.fold_in(key, 103), -4.0, 4.0, (BATCH, BOTTLE), jnp.float32)
    strength = jnp.full((BATCH, 1), 0.85, jnp.float32)
    return (noise + strength * mixture).astype(jnp.bfloat16)


def draw_student_rows(key, part):
    mixture = crop_mixture(key)
    noise = jax.random.truncated_normal(jax.random.fold_in(key, 105), -4.0, 4.0, (BATCH, BOTTLE), jnp.float32)
    strength = jnp.full((BATCH, 1), 0.7, jnp.float32)
    return (noise + strength * mixture).astype(jnp.bfloat16)


def draw_prototypes(key, part):
    centers = center_table(key)
    labels = jax.random.randint(jax.random.fold_in(key, 107), (PROTOTYPES,), 0, 16)
    noise = jax.random.truncated_normal(jax.random.fold_in(key, 108), -4.0, 4.0, (BOTTLE, PROTOTYPES), jnp.float32)
    position = jnp.arange(PROTOTYPES, dtype=jnp.float32)[None, :] / (PROTOTYPES - 1.0)
    strength = 0.2 + 0.8 * position
    return (noise + strength * jnp.transpose(centers[labels])).astype(jnp.bfloat16)


def setup_inputs(seed: int = 0) -> dict:
    streams_of = jax.random.split(jax.random.key(seed), 4)
    teacher_rows = draw_teacher_rows(jax.random.fold_in(streams_of[3], 71), 0)
    student_rows = draw_student_rows(jax.random.fold_in(streams_of[3], 71), 0)
    prototypes = draw_prototypes(jax.random.fold_in(streams_of[3], 71), 0)
    return dict(teacher_rows=teacher_rows, student_rows=student_rows, prototypes=prototypes)


EPSILON = 1e-06
TEACHER_TEMP = 0.04
STUDENT_TEMP = 0.1

def unit_rows(values):
    floats = values.astype(jnp.float32)
    norms = jnp.sqrt(lax.optimization_barrier(jnp.sum(floats * floats, axis=1, keepdims=True)) + EPSILON)
    return (floats / norms, norms)

def reference(teacher_rows, student_rows, prototypes):
    proto_float = prototypes.astype(jnp.float32)
    proto_norm = jnp.sqrt(lax.optimization_barrier(jnp.sum(proto_float * proto_float, axis=0, keepdims=True)) + EPSILON)
    proto_unit = proto_float / proto_norm
    proto_half = proto_unit.astype(jnp.bfloat16)
    teacher_unit = unit_rows(teacher_rows)[0]
    student_float, student_norm = unit_rows(student_rows)
    student_unit = student_float.astype(jnp.bfloat16)
    nblocks = 16
    width = PROTOTYPES // nblocks
    blocks_full = jnp.transpose(proto_unit.reshape(BOTTLE, nblocks, width), (1, 0, 2))
    blocks_half = jnp.transpose(proto_half.reshape(BOTTLE, nblocks, width), (1, 0, 2))

    def teacher_block(block):
        return jnp.exp(jnp.dot(teacher_unit, block, precision=lax.Precision.HIGHEST, preferred_element_type=jnp.float32) / TEACHER_TEMP)

    def student_block(block):
        return jnp.dot(student_unit, block, preferred_element_type=jnp.float32) / STUDENT_TEMP
    weights = jnp.ones((BATCH,), jnp.float32)
    inverse = jnp.ones((PROTOTYPES,), jnp.float32)
    for sweep in range(ITERS):
        columns = lax.map(lambda block: lax.optimization_barrier(jnp.sum(teacher_block(block) * weights[:, None], axis=0)), blocks_full)
        inverse = 1.0 / columns.reshape(PROTOTYPES)
        inverse_blocks = inverse.reshape(nblocks, width)
        partial_rows = lax.map(lambda pair: lax.optimization_barrier(jnp.sum(teacher_block(pair[0]) * pair[1][None, :], axis=1)), (blocks_full, inverse_blocks))
        weights = 1.0 / lax.optimization_barrier(jnp.sum(partial_rows, axis=0))
    totals = lax.map(lambda block: lax.optimization_barrier(jnp.sum(jnp.exp(student_block(block)), axis=1)), blocks_half)
    sample_total = lax.optimization_barrier(jnp.sum(totals, axis=0))
    inverse_blocks = inverse.reshape(nblocks, width)

    def accumulate(carry, triple):
        grad_acc, loss_acc = carry
        block_full, block_half, inv_block = triple
        targets = teacher_block(block_full) * inv_block[None, :] * weights[:, None]
        logits = student_block(block_half)
        signal = (jnp.exp(logits) / sample_total[:, None] - targets).astype(jnp.bfloat16)
        grad_acc = grad_acc + lax.dot_general(signal, block_half, (((1,), (1,)), ((), ())), preferred_element_type=jnp.float32)
        loss_acc = loss_acc + lax.optimization_barrier(jnp.sum(targets * logits, axis=1))
        return ((grad_acc, loss_acc), None)
    start = (jnp.zeros((BATCH, BOTTLE), jnp.float32), jnp.zeros((BATCH,), jnp.float32))
    (grad_sum, cross), unused = lax.scan(accumulate, start, (blocks_full, blocks_half, inverse_blocks))
    direction = grad_sum / STUDENT_TEMP
    radial = lax.optimization_barrier(jnp.sum(student_float * direction, axis=1, keepdims=True))
    row_grads = (direction - student_float * radial) / student_norm
    row_loss = jnp.log(sample_total) - cross
    return (row_grads, row_loss)
```

```python
import functools
import math

import jax
import jax.numpy as jnp
from jax import lax
from jax.experimental import pallas as pl
from jax.experimental.pallas import tpu as pltpu
from jax.sharding import PartitionSpec as P

EPSILON = 1e-06
TEACHER_TEMP = 0.04
STUDENT_TEMP = 0.1
LOG2E = math.log2(math.e)
F32 = jnp.float32
BF16 = jnp.bfloat16
MIB = 1 << 20
NT = (((1,), (1,)), ((), ()))
VMEM = pl.BlockSpec(memory_space=pltpu.VMEM)
PIECES = 8


def call(body, outs, args, scratch=(), vmem=4, flops=0, aliases={}):
    many = isinstance(outs, list)
    made = pl.pallas_call(
        body,
        out_shape=outs,
        in_specs=[VMEM] * len(args),
        out_specs=[VMEM] * len(outs) if many else VMEM,
        scratch_shapes=list(scratch),
        input_output_aliases=aliases,
        compiler_params=pltpu.CompilerParams(vmem_limit_bytes=vmem * MIB),
        cost_estimate=pl.CostEstimate(flops=flops, bytes_accessed=0, transcendentals=0),
    )
    return made(*[pltpu.with_memory_space_constraint(arg, pltpu.VMEM) for arg in args])


def aligned(index, size):
    return pl.ds(pl.multiple_of(index, size), size)


def norms_of(rows):
    floats = rows.astype(F32)
    return floats, jnp.sqrt(jnp.sum(floats * floats, axis=1, keepdims=True) + EPSILON)


def as_column(row):
    size = row.shape[1]
    if size < 128:
        row = jnp.concatenate([row, jnp.zeros((1, 128 - size), F32)], axis=1)
    return jnp.transpose(jnp.broadcast_to(row, (128, 128)))[:size]


def lane_groups(values):
    parts = [values[:, s : s + 128] for s in range(0, values.shape[1], 128)]
    while len(parts) > 1:
        rest = parts[len(parts) // 2 * 2 :]
        parts = [a + b for a, b in zip(parts[::2], parts[1::2])] + rest
    return parts[0]


def wide(column, width):
    return jnp.concatenate([column] * (width // 128), axis=1)


def fold(flat_ref, out_ref):
    for s in range(out_ref.shape[0]):
        out_ref[s : s + 1, :] = flat_ref[:, s * 128 : (s + 1) * 128]


def unfold(values, flat_ref):
    for s in range(values.shape[0]):
        flat_ref[:, s * 128 : (s + 1) * 128] = values[s : s + 1, :]


def rows_out(acc_ref, row_ref):
    for s in range(row_ref.shape[0]):
        block = jnp.transpose(acc_ref[s * 128 : (s + 1) * 128, :])
        row_ref[s : s + 1, :] = jnp.sum(block, axis=0, keepdims=True)


def prep_body(width, p_ref, half_ref, scale_ref):
    def step(i, _):
        cols = aligned(i * width, width)
        floats = p_ref[:, cols].astype(F32)
        scale = lax.rsqrt(jnp.sum(floats * floats, axis=0, keepdims=True) + EPSILON)
        half_ref[:, cols] = (floats * scale).astype(BF16)
        scale_ref[:, cols] = scale
        return 0

    lax.fori_loop(0, p_ref.shape[1] // width, step, 0)


def exp_body(width, chunk, slots, *refs):
    parts, (p_ref, scale_ref, e_ref, col_ref, unit_ref, t_ref, a_ref, flat_ref) = refs[:slots], refs[slots:]
    rows, cols_all = e_ref.shape
    size = rows // slots
    for m, part in enumerate(parts):
        here = slice(m * size, (m + 1) * size)
        teacher = part[0:size, :]
        t_ref[here, :] = teacher
        a_ref[here, :] = jnp.broadcast_to((LOG2E / TEACHER_TEMP) / norms_of(teacher)[1], (size, 128))
        floats, norm = norms_of(part[size:, :])
        unit_ref[here, :] = (floats / norm).astype(BF16)

    def step(i, _):
        for n in range(width // 256):
            cols = aligned(i * width + n * 256, 256)
            p = p_ref[:, cols]
            scale = scale_ref[:, cols]
            acc = jnp.zeros((8, 256), F32)
            for r in range(0, rows, chunk):
                d = jnp.dot(t_ref[r : r + chunk, :], p, preferred_element_type=F32)
                e = jnp.exp2(d * wide(a_ref[r : r + chunk, :], 256) * scale)
                e_ref[r : r + chunk, cols] = e.astype(BF16)
                acc = acc + jnp.sum(e.reshape(chunk // 8, 8, 256), axis=0)
            flat_ref[:, cols] = jnp.sum(acc, axis=0, keepdims=True)
        return 0

    lax.fori_loop(0, cols_all // width, step, 0)
    fold(flat_ref, col_ref)


def rowsum_body(width, group, chunk, core_lanes, e_ref, one_ref, two_ref, inv_ref, row_ref, swap_ref, acc_ref, flat_ref):
    rows, cols_all = e_ref.shape
    inv = 1.0 / (one_ref[...] + two_ref[...])
    inv_ref[...] = inv
    unfold(inv, flat_ref)
    acc_ref[...] = jnp.zeros_like(acc_ref)

    def step(i, _):
        for r in range(0, rows, chunk):
            acc = acc_ref[r : r + chunk, :]
            for n in range(width // group):
                cols = aligned(i * width + n * group, group)
                acc = acc + lane_groups(e_ref[r : r + chunk, cols].astype(F32) * flat_ref[:, cols])
            acc_ref[r : r + chunk, :] = acc
        return 0

    lax.fori_loop(0, cols_all // width, step, 0)
    rows_out(acc_ref, row_ref)
    if core_lanes == 128:
        for s in range(row_ref.shape[0]):
            swap_ref[s : s + 1, :] = row_ref[s ^ 1 : (s ^ 1) + 1, :]
    else:
        held = row_ref[...]
        swap_ref[...] = jnp.concatenate([held[:, core_lanes:], held[:, :core_lanes]], axis=1)


def colsum_body(width, size, e_ref, *refs):
    parts, (col_ref, w_ref, flat_ref) = refs[:-3], refs[-3:]
    rows, cols_all = e_ref.shape
    for s in range(rows // 128):
        total = parts[0][s : s + 1, :]
        for j, part in enumerate(parts[1:], 1):
            from_ = s ^ (2 * j * size // 128)
            total = total + part[from_ : from_ + 1, :]
        w = 1.0 / total
        high = w.astype(BF16).astype(F32)
        low = w - high
        both = jnp.concatenate([high, low, jnp.zeros((14, 128), F32)], axis=0)
        w_ref[:, s * 128 : (s + 1) * 128] = both.astype(BF16)

    def step(i, _):
        cols = aligned(i * width, width)
        sums = jnp.dot(w_ref[...], e_ref[:, cols], preferred_element_type=F32)
        flat_ref[:, cols] = sums[0:1, :] + sums[1:2, :]
        return 0

    lax.fori_loop(0, cols_all // width, step, 0)
    fold(flat_ref, col_ref)


def student_body(width, group, chunk, first, last, unit_ref, half_ref, *refs):
    grad_ref, acc_ref = refs[-2:]
    rows = unit_ref.shape[0]
    if first == 0:
        grad_ref[...] = jnp.zeros_like(grad_ref)
        acc_ref[...] = jnp.zeros_like(acc_ref)

    def step(i, _):
        for n in range(width // group):
            cols = aligned(first + i * width + n * group, group)
            q = half_ref[:, cols]
            for r in range(0, rows, chunk):
                d = jnp.dot(unit_ref[r : r + chunk, :], q, preferred_element_type=F32)
                x = jnp.exp2(d * (LOG2E / STUDENT_TEMP))
                grad_ref[r : r + chunk, :] += lax.dot_general(x.astype(BF16), q, NT, preferred_element_type=F32)
                acc_ref[r : r + chunk, :] += lane_groups(x)
        return 0

    lax.fori_loop(0, (last - first) // width, step, 0)


def last_body(width, chunk, slots, e_ref, inv_ref, half_ref, row_ref, grad_ref, sum_ref, even_ref, odd_ref, b_ref, flat_ref, s_ref):
    rows, cols_all = e_ref.shape
    size = rows // slots
    unfold(inv_ref[...], flat_ref)
    rows_out(sum_ref, s_ref)
    b_ref[...] = jnp.zeros_like(b_ref)

    def step(i, _):
        cols = aligned(i * width, width)
        q = (half_ref[:, cols].astype(F32) * flat_ref[:, cols]).astype(BF16)
        for r in range(0, rows, chunk):
            b_ref[r : r + chunk, :] += lax.dot_general(e_ref[r : r + chunk, cols], q, NT, preferred_element_type=F32)
        return 0

    lax.fori_loop(0, cols_all // width, step, 0)
    depth = grad_ref.shape[1]
    for m in range(slots):
        out = odd_ref if m % 2 else even_ref
        here = slice(m * size, (m + 1) * size)
        out[m // 2, 0:size, 0:depth] = grad_ref[here, :]
        out[m // 2, 0:size, depth:] = b_ref[here, :]
        out[m // 2, size:, :] = jnp.zeros((8, 2 * depth), F32)
        s, lane = divmod(m * size, 128)
        out[m // 2, size : size + 1, 0:size] = s_ref[s : s + 1, lane : lane + size]
        out[m // 2, size : size + 1, depth : depth + size] = row_ref[s : s + 1, lane : lane + size]


def final_body(student_ref, *refs):
    parts, (grads_ref, loss_ref) = refs[:-2], refs[-2:]
    size, depth = student_ref.shape
    total = parts[0][...]
    for part in parts[1:]:
        total = total + part[...]
    s_row = total[size : size + 1, 0:size]
    r_row = total[size : size + 1, depth : depth + size]
    a = total[0:size, 0:depth] / wide(as_column(s_row), depth)
    b = total[0:size, depth:] / wide(as_column(r_row), depth)
    floats, norm = norms_of(student_ref[...])
    unit = floats / norm
    direction = (a - b) / STUDENT_TEMP
    radial = jnp.sum(unit * direction, axis=1, keepdims=True)
    grads_ref[...] = (direction - unit * radial) / norm
    product = unit.astype(BF16).astype(F32) * b
    cross = jnp.sum(product, axis=1, keepdims=True) / STUDENT_TEMP
    cross = jnp.broadcast_to(cross, (size, 128))
    if size < 128:
        cross = jnp.concatenate([cross, jnp.zeros((128 - size, 128), F32)], axis=0)
    loss_ref[...] = jnp.log(s_row) - jnp.transpose(cross)[0:1, 0:size]


def on_device(row_devices, proto_devices, teacher_rows, student_rows, prototypes):
    size, depth = teacher_rows.shape
    cols = prototypes.shape[1]
    rows = size * proto_devices
    chips = range(2, proto_devices, 2)
    lines, blocks = rows // 128, cols // 128
    vm = pltpu.VMEM

    def swap(values, mask, axis="protos", count=proto_devices):
        return lax.ppermute(values, axis, [(i, i ^ mask) for i in range(count)])

    def over_rows(values):
        mask = 1
        while True:
            other = swap(values, mask, "rows", row_devices)
            mask *= 2
            if mask >= row_devices:
                return values, other
            values = values + other

    both = jnp.concatenate([teacher_rows, student_rows], axis=0)
    even = [both] + [swap(both, mask) for mask in chips]
    odd = [swap(part, 1) for part in even]
    parts = [part for pair in zip(even, odd) for part in pair]

    half, scale = call(functools.partial(prep_body, 512), [vm((depth, cols), BF16), vm((1, cols), F32)], [prototypes])
    exps, col, unit = call(
        functools.partial(exp_body, 2048, 256, proto_devices),
        [vm((rows, cols), BF16), vm((blocks, 128), F32), vm((rows, depth), BF16)],
        parts + [prototypes, scale],
        [pltpu.VMEM((rows, depth), BF16), pltpu.VMEM((rows, 128), F32), pltpu.VMEM((1, cols), F32)],
        vmem=6,
    )

    work = 4 * rows * cols * depth // PIECES

    def student(piece, held):
        first, last = piece * cols // PIECES, (piece + 1) * cols // PIECES
        return call(
            functools.partial(student_body, min(2048, last - first), 1024, 256, first, last),
            [vm((rows, depth), F32), vm((rows, 128), F32)],
            [unit, half, *held],
            vmem=6,
            flops=work,
            aliases={2: 0, 3: 1} if held else {},
        )

    held = []
    for piece in range(PIECES):
        held = student(piece, held)

    for sweep in range(3):
        one, two = over_rows(col)
        inv, row, swapped = call(
            functools.partial(rowsum_body, 2048, 1024, 128, size),
            [vm((blocks, 128), F32), vm((lines, 128), F32), vm((lines, 128), F32)],
            [exps, one, two],
            [pltpu.VMEM((rows, 128), F32), pltpu.VMEM((1, cols), F32)],
        )
        if sweep == 2:
            break
        row = row + swap(swapped, 1)
        col = call(
            functools.partial(colsum_body, 4096, size),
            vm((blocks, 128), F32),
            [exps, row] + [swap(row, mask) for mask in chips],
            [pltpu.VMEM((16, rows), BF16), pltpu.VMEM((1, cols), F32)],
        )

    block = vm((proto_devices // 2, size + 8, 2 * depth), F32)
    stay, leave = call(
        functools.partial(last_body, 2048, 256, proto_devices),
        [block, block],
        [exps, inv, half, row, *held],
        [pltpu.VMEM((rows, depth), F32), pltpu.VMEM((1, cols), F32), pltpu.VMEM((lines, 128), F32)],
        vmem=6,
    )
    stay = stay + swap(leave, 1)
    sums = [stay[0]] + [swap(stay[mask // 2], mask) for mask in chips]
    grads, loss = call(
        final_body,
        [jax.ShapeDtypeStruct((size, depth), F32), jax.ShapeDtypeStruct((1, size), F32)],
        [student_rows] + sums,
    )
    return grads, loss.reshape(size)


def solution(mesh):
    in_specs = (P(("rows", "protos"), None), P(("rows", "protos"), None), P(None, "protos"))
    out_specs = (P(("rows", "protos"), None), P(("rows", "protos")))
    return jax.shard_map(
        functools.partial(on_device, mesh.shape["rows"], mesh.shape["protos"]),
        mesh=mesh,
        in_specs=in_specs,
        out_specs=out_specs,
        check_vma=False,
    )
```

```python
import functools
import math

import jax
import jax.numpy as jnp
from jax import lax
from jax.experimental import pallas as pl
from jax.experimental.pallas import tpu as pltpu
from jax.sharding import PartitionSpec as P

EPSILON = 1e-06
TEACHER_TEMP = 0.04
STUDENT_TEMP = 0.1
LOG2E = math.log2(math.e)
F32 = jnp.float32
BF16 = jnp.bfloat16
MIB = 1 << 20
NT = (((1,), (1,)), ((), ()))
VMEM = pl.BlockSpec(memory_space=pltpu.VMEM)
HBM = pl.BlockSpec(memory_space=pltpu.HBM)
PIECES = 8
PARTS = 4


def call(body, outs, args, scratch=(), vmem=4, flops=0, aliases={}, streamed=()):
    many = isinstance(outs, list)
    places = [HBM if i in streamed else VMEM for i in range(len(args))]
    made = pl.pallas_call(
        body,
        out_shape=outs,
        in_specs=places,
        out_specs=[VMEM] * len(outs) if many else VMEM,
        scratch_shapes=list(scratch),
        input_output_aliases=aliases,
        compiler_params=pltpu.CompilerParams(vmem_limit_bytes=vmem * MIB),
        cost_estimate=pl.CostEstimate(flops=flops, bytes_accessed=0, transcendentals=0),
    )
    spaces = [pltpu.HBM if i in streamed else pltpu.VMEM for i in range(len(args))]
    return made(*map(pltpu.with_memory_space_constraint, args, spaces))


def aligned(index, size):
    return pl.ds(pl.multiple_of(index, size), size)


def norms_of(rows):
    floats = rows.astype(F32)
    return floats, jnp.sqrt(jnp.sum(floats * floats, axis=1, keepdims=True) + EPSILON)


def as_column(row):
    size = row.shape[1]
    if size < 128:
        row = jnp.concatenate([row, jnp.zeros((1, 128 - size), F32)], axis=1)
    return jnp.transpose(jnp.broadcast_to(row, (128, 128)))[:size]


def lane_groups(values):
    parts = [values[:, s : s + 128] for s in range(0, values.shape[1], 128)]
    while len(parts) > 1:
        rest = parts[len(parts) // 2 * 2 :]
        parts = [a + b for a, b in zip(parts[::2], parts[1::2])] + rest
    return parts[0]


def wide(column, width):
    return jnp.concatenate([column] * (width // 128), axis=1)


def fold(flat_ref, out_ref):
    for s in range(out_ref.shape[0]):
        out_ref[s : s + 1, :] = flat_ref[:, s * 128 : (s + 1) * 128]


def unfold(values, flat_ref):
    for s in range(values.shape[0]):
        flat_ref[:, s * 128 : (s + 1) * 128] = values[s : s + 1, :]


def rows_out(acc_ref, row_ref):
    for s in range(row_ref.shape[0]):
        block = jnp.transpose(acc_ref[s * 128 : (s + 1) * 128, :])
        row_ref[s : s + 1, :] = jnp.sum(block, axis=0, keepdims=True)


def prep_body(p_ref, half_ref, scale_ref):
    floats = p_ref[...].astype(F32)
    scale = lax.rsqrt(jnp.sum(floats * floats, axis=0, keepdims=True) + EPSILON)
    half_ref[...] = (floats * scale).astype(BF16)
    scale_ref[...] = scale


def prep(prototypes, width):
    depth, cols = prototypes.shape

    def block(rows):
        return pl.BlockSpec((rows, width), lambda i: (0, i))

    return pl.pallas_call(
        prep_body,
        grid=(cols // width,),
        out_shape=[pltpu.HBM((depth, cols), BF16), jax.ShapeDtypeStruct((1, cols), F32)],
        in_specs=[block(depth)],
        out_specs=[block(depth), block(1)],
        compiler_params=pltpu.CompilerParams(vmem_limit_bytes=8 * MIB),
        cost_estimate=pl.CostEstimate(flops=8 * depth * cols, bytes_accessed=4 * depth * cols, transcendentals=0),
    )(pltpu.with_memory_space_constraint(prototypes, pltpu.HBM))


def stream(source_ref, held_ref, sem_ref, width, steps, work):
    def copy(i):
        slot = lax.rem(i, 2)
        return pltpu.make_async_copy(source_ref.at[:, aligned(i * width, width)], held_ref.at[slot], sem_ref.at[slot])

    total = steps * len(work)
    copy(0).start()
    for k, part in enumerate(work):

        def step(i, _, k=k, part=part):
            at = k * steps + i

            @pl.when(at + 1 < total)
            def _():
                copy(at + 1).start()

            copy(at).wait()
            part(i, lax.rem(at, 2))
            return 0

        lax.fori_loop(0, steps, step, 0)


def exp_body(width, chunk, slots, *refs):
    parts, (p_ref, scale_ref), e_refs = refs[:slots], refs[slots : slots + 2], refs[slots + 2 : -7]
    col_ref, unit_ref, t_ref, a_ref, flat_ref, p_held, p_sem = refs[-7:]
    rows, span = e_refs[0].shape
    size = rows // slots
    for m, part in enumerate(parts):
        here = slice(m * size, (m + 1) * size)
        teacher = part[0:size, :]
        t_ref[here, :] = teacher
        a_ref[here, :] = jnp.broadcast_to((LOG2E / TEACHER_TEMP) / norms_of(teacher)[1], (size, 128))
        floats, norm = norms_of(part[size:, :])
        unit_ref[here, :] = (floats / norm).astype(BF16)

    def step(first, e_ref, i, slot):
        for n in range(width // 256):
            here = aligned(i * width + n * 256, 256)
            cols = aligned(first + i * width + n * 256, 256)
            p = p_held[slot, :, n * 256 : (n + 1) * 256]
            scale = scale_ref[:, cols]
            acc = jnp.zeros((8, 256), F32)
            for r in range(0, rows, chunk):
                d = jnp.dot(t_ref[r : r + chunk, :], p, preferred_element_type=F32)
                e = jnp.exp2(d * wide(a_ref[r : r + chunk, :], 256) * scale)
                e_ref[r : r + chunk, here] = e.astype(BF16)
                acc = acc + jnp.sum(e.reshape(chunk // 8, 8, 256), axis=0)
            flat_ref[:, cols] = jnp.sum(acc, axis=0, keepdims=True)

    works = [functools.partial(step, k * span, e_ref) for k, e_ref in enumerate(e_refs)]
    stream(p_ref, p_held, p_sem, width, span // width, works)
    fold(flat_ref, col_ref)


def rowsum_body(width, group, chunk, *refs):
    e_refs, (one_ref, two_ref, inv_ref, row_ref, swap_ref, acc_ref, flat_ref) = refs[:-7], refs[-7:]
    rows, span = e_refs[0].shape
    inv = 1.0 / (one_ref[...] + two_ref[...])
    inv_ref[...] = inv
    unfold(inv, flat_ref)
    acc_ref[...] = jnp.zeros_like(acc_ref)

    def step(first, e_ref, i, _):
        for r in range(0, rows, chunk):
            acc = acc_ref[r : r + chunk, :]
            for n in range(width // group):
                here = aligned(i * width + n * group, group)
                cols = aligned(first + i * width + n * group, group)
                acc = acc + lane_groups(e_ref[r : r + chunk, here].astype(F32) * flat_ref[:, cols])
            acc_ref[r : r + chunk, :] = acc
        return 0

    for k, e_ref in enumerate(e_refs):
        lax.fori_loop(0, span // width, functools.partial(step, k * span, e_ref), 0)
    rows_out(acc_ref, row_ref)
    middle = row_ref.shape[0] // 2
    swap_ref[0:middle, :] = row_ref[middle:, :]
    swap_ref[middle:, :] = row_ref[0:middle, :]


def colsum_body(width, size, count, *refs):
    e_refs, parts, (col_ref, w_ref, flat_ref) = refs[:count], refs[count:-3], refs[-3:]
    rows, span = e_refs[0].shape
    for s in range(rows // 128):
        total = parts[0][s : s + 1, :]
        for j, part in enumerate(parts[1:], 1):
            line, lane = divmod(j * size, 128)
            other = part[s ^ line : (s ^ line) + 1, :]
            if lane:
                other = jnp.concatenate([other[:, lane:], other[:, :lane]], axis=1)
            total = total + other
        w = 1.0 / total
        high = w.astype(BF16).astype(F32)
        low = w - high
        both = jnp.concatenate([high, low, jnp.zeros((14, 128), F32)], axis=0)
        w_ref[:, s * 128 : (s + 1) * 128] = both.astype(BF16)

    def step(first, e_ref, i, _):
        sums = jnp.dot(w_ref[...], e_ref[:, aligned(i * width, width)], preferred_element_type=F32)
        flat_ref[:, aligned(first + i * width, width)] = sums[0:1, :] + sums[1:2, :]
        return 0

    for k, e_ref in enumerate(e_refs):
        lax.fori_loop(0, span // width, functools.partial(step, k * span, e_ref), 0)
    fold(flat_ref, col_ref)


def student_body(width, chunk, fresh, first, last, unit_ref, half_ref, *refs):
    grad_ref, acc_ref, held, sem = refs[-4:]
    rows = unit_ref.shape[0]
    if fresh:
        grad_ref[...] = jnp.zeros_like(grad_ref)
        acc_ref[...] = jnp.zeros_like(acc_ref)

    def step(i, slot):
        q = held[slot]
        for r in range(0, rows, chunk):
            d = jnp.dot(unit_ref[r : r + chunk, :], q, preferred_element_type=F32)
            x = jnp.exp2(d * (LOG2E / STUDENT_TEMP))
            grad_ref[r : r + chunk, :] += lax.dot_general(x.astype(BF16), q, NT, preferred_element_type=F32)
            acc_ref[r : r + chunk, :] += lane_groups(x)

    source = half_ref.at[:, first:last]
    stream(source, held, sem, width, (last - first) // width, [step])


def gather_body(width, chunk, first, size, depth, *refs):
    e_refs, (inv_ref, half_ref, row_ref, out_ref, b_ref, flat_ref, held, sem) = refs[:-8], refs[-8:]
    span = e_refs[0].shape[1]
    rows = b_ref.shape[0]
    unfold(inv_ref[...], flat_ref)
    b_ref[...] = jnp.zeros_like(b_ref)

    def step(start, e_ref, i, slot):
        here = aligned(i * width, width)
        cols = aligned(start + i * width, width)
        q = (held[slot].astype(F32) * flat_ref[:, cols]).astype(BF16)
        for r in range(0, rows, chunk):
            e = e_ref[first + r : first + r + chunk, here]
            b_ref[r : r + chunk, :] += lax.dot_general(e, q, NT, preferred_element_type=F32)

    works = [functools.partial(step, k * span, e_ref) for k, e_ref in enumerate(e_refs)]
    stream(half_ref, held, sem, width, span // width, works)
    blocks_out(b_ref, 0, row_ref, first, size, out_ref)


def blocks_out(values_ref, start, row_ref, first, size, out_ref):
    for j in range(out_ref.shape[0]):
        out_ref[j, 0:size, :] = values_ref[start + j * size : start + (j + 1) * size, :]
        out_ref[j, size:, :] = jnp.zeros((8, out_ref.shape[2]), F32)
        s, lane = divmod(first + j * size, 128)
        out_ref[j, size : size + 1, 0:size] = row_ref[s : s + 1, lane : lane + size]


def pack_body(size, grad_ref, sum_ref, stay_ref, leave_ref, s_ref):
    rows_out(sum_ref, s_ref)
    middle = grad_ref.shape[0] // 2
    blocks_out(grad_ref, 0, s_ref, 0, size, stay_ref)
    blocks_out(grad_ref, middle, s_ref, middle, size, leave_ref)


def final_body(count, student_ref, *refs):
    (grads_ref, loss_ref) = refs[-2:]
    size, depth = student_ref.shape

    def total_of(parts):
        total = parts[0][...]
        for part in parts[1:]:
            total = total + part[...]
        line = total[size : size + 1, 0:size]
        return total[0:size, :] / wide(as_column(line), depth), line

    a, s_row = total_of(refs[:count])
    b, _ = total_of(refs[count:-2])
    floats, norm = norms_of(student_ref[...])
    unit = floats / norm
    direction = (a - b) / STUDENT_TEMP
    radial = jnp.sum(unit * direction, axis=1, keepdims=True)
    grads_ref[...] = (direction - unit * radial) / norm
    product = unit.astype(BF16).astype(F32) * b
    cross = jnp.sum(product, axis=1, keepdims=True) / STUDENT_TEMP
    cross = jnp.broadcast_to(cross, (size, 128))
    if size < 128:
        cross = jnp.concatenate([cross, jnp.zeros((128 - size, 128), F32)], axis=0)
    loss_ref[...] = jnp.log(s_row) - jnp.transpose(cross)[0:1, 0:size]


def on_device(row_devices, proto_devices, teacher_rows, student_rows, prototypes):
    size, depth = teacher_rows.shape
    cols = prototypes.shape[1]
    rows = size * proto_devices
    chips = range(2, proto_devices, 2)
    lines, blocks = rows // 128, cols // 128
    vm = pltpu.VMEM

    def swap(values, mask, axis="protos", count=proto_devices):
        return lax.ppermute(values, axis, [(i, i ^ mask) for i in range(count)])

    def over_rows(values):
        mask = 1
        while True:
            other = swap(values, mask, "rows", row_devices)
            mask *= 2
            if mask >= row_devices:
                return values, other
            values = values + other

    both = jnp.concatenate([teacher_rows, student_rows], axis=0)
    even = [both] + [swap(both, mask) for mask in chips]
    odd = [swap(part, 1) for part in even]

    half, scale = prep(prototypes, 2048)
    *exps, col, unit = call(
        functools.partial(exp_body, 2048, 256, proto_devices),
        [vm((rows, cols // PARTS), BF16)] * PARTS + [vm((blocks, 128), F32), vm((rows, depth), BF16)],
        even + odd + [prototypes, scale],
        [
            pltpu.VMEM((rows, depth), BF16),
            pltpu.VMEM((rows, 128), F32),
            pltpu.VMEM((1, cols), F32),
            pltpu.VMEM((2, depth, 2048), BF16),
            pltpu.SemaphoreType.DMA((2,)),
        ],
        vmem=6,
        streamed=(proto_devices,),
    )

    work = 4 * rows * cols * depth // PIECES

    def student(piece, held):
        first, last = piece * cols // PIECES, (piece + 1) * cols // PIECES
        return call(
            functools.partial(student_body, 1024, 256, not held, first, last),
            [vm((rows, depth), F32), vm((rows, 128), F32)],
            [unit, half, *held],
            [pltpu.VMEM((2, depth, 1024), BF16), pltpu.SemaphoreType.DMA((2,))],
            vmem=6,
            flops=work,
            aliases={2: 0, 3: 1} if held else {},
            streamed=(1,),
        )

    held = []
    for piece in range(PIECES):
        held = student(piece, held)

    for sweep in range(3):
        one, two = over_rows(col)
        inv, row, swapped = call(
            functools.partial(rowsum_body, 2048, 1024, 128),
            [vm((blocks, 128), F32), vm((lines, 128), F32), vm((lines, 128), F32)],
            [*exps, one, two],
            [pltpu.VMEM((rows, 128), F32), pltpu.VMEM((1, cols), F32)],
        )
        if sweep == 2:
            break
        row = row + swap(swapped, 1)
        col = call(
            functools.partial(colsum_body, 4096, size, PARTS),
            vm((blocks, 128), F32),
            [*exps, row] + [swap(row, mask) for mask in chips],
            [pltpu.VMEM((16, rows), BF16), pltpu.VMEM((1, cols), F32)],
        )

    def reduced(stay, leave):
        sums = stay + swap(leave, 1)
        return [sums[0]] + [swap(sums[mask // 2], mask) for mask in chips]

    block = vm((proto_devices // 2, size + 8, depth), F32)
    a_sums = reduced(*call(functools.partial(pack_body, size), [block, block], held, [pltpu.VMEM((lines, 128), F32)]))

    def gathered(first):
        return call(
            functools.partial(gather_body, 2048, 256, first, size, depth),
            block,
            [*exps, inv, half, row],
            [
                pltpu.VMEM((rows // 2, depth), F32),
                pltpu.VMEM((1, cols), F32),
                pltpu.VMEM((2, depth, 2048), BF16),
                pltpu.SemaphoreType.DMA((2,)),
            ],
            vmem=6,
            flops=rows * cols * depth,
            streamed=(PARTS + 1,),
        )

    leave = gathered(rows // 2)
    b_sums = reduced(gathered(0), leave)
    grads, loss = call(
        functools.partial(final_body, proto_devices // 2),
        [jax.ShapeDtypeStruct((size, depth), F32), jax.ShapeDtypeStruct((1, size), F32)],
        [student_rows] + a_sums + b_sums,
    )
    return grads, loss.reshape(size)


def solution(mesh):
    in_specs = (P(("rows", "protos"), None), P(("rows", "protos"), None), P(None, "protos"))
    out_specs = (P(("rows", "protos"), None), P(("rows", "protos")))
    return jax.shard_map(
        functools.partial(on_device, mesh.shape["rows"], mesh.shape["protos"]),
        mesh=mesh,
        in_specs=in_specs,
        out_specs=out_specs,
        check_vma=False,
    )
```

```python
import functools
import math

import jax
import jax.numpy as jnp
from jax import lax
from jax.experimental import pallas as pl
from jax.experimental.pallas import tpu as pltpu
from jax.sharding import PartitionSpec as P

EPSILON = 1e-06
TEACHER_TEMP = 0.04
STUDENT_TEMP = 0.1
LOG2E = math.log2(math.e)
F32 = jnp.float32
BF16 = jnp.bfloat16
MIB = 1 << 20
NT = (((1,), (1,)), ((), ()))
VMEM = pl.BlockSpec(memory_space=pltpu.VMEM)
HBM = pl.BlockSpec(memory_space=pltpu.HBM)
BLOCKS = 16
PIECES = (2, 2, 1, 2, 2, 2, 1, 1, 2, 1)
PARTS = 4
KEPT = BLOCKS // PARTS


def call(body, outs, args, scratch=(), vmem=4, flops=0, aliases={}, streamed=(), streamed_out=()):
    many = isinstance(outs, list)
    places = [HBM if i in streamed else VMEM for i in range(len(args))]
    made = pl.pallas_call(
        body,
        out_shape=outs,
        in_specs=places,
        out_specs=[HBM if i in streamed_out else VMEM for i in range(len(outs))] if many else VMEM,
        scratch_shapes=list(scratch),
        input_output_aliases=aliases,
        compiler_params=pltpu.CompilerParams(vmem_limit_bytes=vmem * MIB),
        cost_estimate=pl.CostEstimate(flops=flops, bytes_accessed=0, transcendentals=0),
    )
    spaces = [pltpu.HBM if i in streamed else pltpu.VMEM for i in range(len(args))]
    return made(*map(pltpu.with_memory_space_constraint, args, spaces))


def aligned(index, size):
    return pl.ds(pl.multiple_of(index, size), size)


def norms_of(rows):
    floats = rows.astype(F32)
    return floats, jnp.sqrt(jnp.sum(floats * floats, axis=1, keepdims=True) + EPSILON)


def as_column(row):
    size = row.shape[1]
    if size < 128:
        row = jnp.concatenate([row, jnp.zeros((1, 128 - size), F32)], axis=1)
    return jnp.transpose(jnp.broadcast_to(row, (128, 128)))[:size]


def lane_groups(values):
    parts = [values[:, s : s + 128] for s in range(0, values.shape[1], 128)]
    while len(parts) > 1:
        rest = parts[len(parts) // 2 * 2 :]
        parts = [a + b for a, b in zip(parts[::2], parts[1::2])] + rest
    return parts[0]


def wide(column, width):
    return jnp.concatenate([column] * (width // 128), axis=1)


def fold(flat_ref, out_ref):
    for s in range(out_ref.shape[0]):
        out_ref[s : s + 1, :] = flat_ref[:, s * 128 : (s + 1) * 128]


def unfold(values, flat_ref):
    for s in range(values.shape[0]):
        flat_ref[:, s * 128 : (s + 1) * 128] = values[s : s + 1, :]


def rows_out(acc_ref, row_ref):
    for s in range(row_ref.shape[0]):
        block = jnp.transpose(acc_ref[s * 128 : (s + 1) * 128, :])
        row_ref[s : s + 1, :] = jnp.sum(block, axis=0, keepdims=True)


def stream(source_refs, held_ref, sem_ref, width, work):
    steps = source_refs[0].shape[1] // width

    def copy(source_ref, i, slot):
        return pltpu.make_async_copy(source_ref.at[:, aligned(i * width, width)], held_ref.at[slot], sem_ref.at[slot])

    copy(source_refs[0], 0, 0).start()
    for k, source_ref in enumerate(source_refs):

        def step(i, _, k=k, source_ref=source_ref):
            slot, other = lax.rem(k * steps + i, 2), lax.rem(k * steps + i + 1, 2)

            @pl.when(i + 1 < steps)
            def _():
                copy(source_ref, i + 1, other).start()

            if k + 1 < len(source_refs):

                @pl.when(i + 1 == steps)
                def _():
                    copy(source_refs[k + 1], 0, other).start()

            copy(source_ref, i, slot).wait()
            work[k](i, slot)
            return 0

        lax.fori_loop(0, steps, step, 0)


def exp_body(width, chunk, slots, *refs):
    parts, p_ref, refs = refs[:slots], refs[slots], refs[slots + 1 :]
    e_refs, kept_ref, half_refs, refs = refs[:PARTS], refs[PARTS], refs[PARTS + 1 :][: BLOCKS - KEPT], refs[PARTS + 1 + BLOCKS - KEPT :]
    col_ref, unit_ref, scale_ref, t_ref, a_ref, flat_ref, p_held, p_sem, out, out_sem = refs
    rows, span = e_refs[0].shape
    size = rows // slots
    for m, part in enumerate(parts):
        here = slice(m * size, (m + 1) * size)
        teacher = part[0:size, :]
        t_ref[here, :] = teacher
        a_ref[here, :] = jnp.broadcast_to((LOG2E / TEACHER_TEMP) / norms_of(teacher)[1], (size, 128))
        floats, norm = norms_of(part[size:, :])
        unit_ref[here, :] = (floats / norm).astype(BF16)

    steps, block = span // width, half_refs[0].shape[1]

    def copies(at):
        slot, count = at % steps, width // block
        return [
            pltpu.make_async_copy(
                out.at[slot, :, q * block : (q + 1) * block], half_refs[at * count + q], out_sem.at[slot, q]
            )
            for q in range(count)
        ]

    def step(k, e_ref, i, slot):
        first = k * span
        if k > 1:
            for q in range(steps):

                @pl.when(i == q)
                def _(q=q):
                    for copy in copies((k - 2) * steps + q):
                        copy.wait()

        for n in range(width // 256):
            here = aligned(i * width + n * 256, 256)
            cols = aligned(first + i * width + n * 256, 256)
            p = p_held[slot, :, n * 256 : (n + 1) * 256]
            floats = p.astype(F32)
            scale = lax.rsqrt(jnp.sum(floats * floats, axis=0, keepdims=True) + EPSILON)
            half = (floats * scale).astype(BF16)
            if k:
                out[i, :, n * 256 : (n + 1) * 256] = half
            else:
                kept_ref[:, here] = half
            scale_ref[:, cols] = scale
            acc = jnp.zeros((8, 256), F32)
            for r in range(0, rows, chunk):
                d = jnp.dot(t_ref[r : r + chunk, :], p, preferred_element_type=F32)
                e = jnp.exp2(d * wide(a_ref[r : r + chunk, :], 256) * scale)
                e_ref[r : r + chunk, here] = e.astype(BF16)
                acc = acc + jnp.sum(e.reshape(chunk // 8, 8, 256), axis=0)
            flat_ref[:, cols] = jnp.sum(acc, axis=0, keepdims=True)
        for q in range(steps if k else 0):

            @pl.when(i == q)
            def _(q=q):
                for copy in copies((k - 1) * steps + q):
                    copy.start()

    works = [functools.partial(step, k, e_ref) for k, e_ref in enumerate(e_refs)]
    stream([p_ref.at[:, k * span : (k + 1) * span] for k in range(PARTS)], p_held, p_sem, width, works)
    fold(flat_ref, col_ref)
    for q in range(steps):
        for copy in copies((PARTS - 2) * steps + q):
            copy.wait()


def rowsum_body(width, group, chunk, *refs):
    e_refs, (one_ref, two_ref, inv_ref, row_ref, swap_ref, acc_ref, flat_ref) = refs[:-7], refs[-7:]
    rows, span = e_refs[0].shape
    inv = 1.0 / (one_ref[...] + two_ref[...])
    inv_ref[...] = inv
    unfold(inv, flat_ref)
    acc_ref[...] = jnp.zeros_like(acc_ref)

    def step(first, e_ref, i, _):
        for r in range(0, rows, chunk):
            acc = acc_ref[r : r + chunk, :]
            for n in range(width // group):
                here = aligned(i * width + n * group, group)
                cols = aligned(first + i * width + n * group, group)
                acc = acc + lane_groups(e_ref[r : r + chunk, here].astype(F32) * flat_ref[:, cols])
            acc_ref[r : r + chunk, :] = acc
        return 0

    for k, e_ref in enumerate(e_refs):
        lax.fori_loop(0, span // width, functools.partial(step, k * span, e_ref), 0)
    rows_out(acc_ref, row_ref)
    middle = row_ref.shape[0] // 2
    swap_ref[0:middle, :] = row_ref[middle:, :]
    swap_ref[middle:, :] = row_ref[0:middle, :]


def colsum_body(width, size, count, *refs):
    e_refs, parts, (col_ref, w_ref, flat_ref) = refs[:count], refs[count:-3], refs[-3:]
    rows, span = e_refs[0].shape
    for s in range(rows // 128):
        total = parts[0][s : s + 1, :]
        for j, part in enumerate(parts[1:], 1):
            line, lane = divmod(j * size, 128)
            other = part[s ^ line : (s ^ line) + 1, :]
            if lane:
                other = jnp.concatenate([other[:, lane:], other[:, :lane]], axis=1)
            total = total + other
        w = 1.0 / total
        high = w.astype(BF16).astype(F32)
        low = w - high
        both = jnp.concatenate([high, low, jnp.zeros((14, 128), F32)], axis=0)
        w_ref[:, s * 128 : (s + 1) * 128] = both.astype(BF16)

    def step(first, e_ref, i, _):
        sums = jnp.dot(w_ref[...], e_ref[:, aligned(i * width, width)], preferred_element_type=F32)
        flat_ref[:, aligned(first + i * width, width)] = sums[0:1, :] + sums[1:2, :]
        return 0

    for k, e_ref in enumerate(e_refs):
        lax.fori_loop(0, span // width, functools.partial(step, k * span, e_ref), 0)
    fold(flat_ref, col_ref)


def student_body(chunk, fresh, span, starts, unit_ref, *refs):
    half_refs, (grad_ref, acc_ref) = refs[: len(starts)], refs[-2:]
    rows = unit_ref.shape[0]
    if fresh:
        grad_ref[...] = jnp.zeros_like(grad_ref)
        acc_ref[...] = jnp.zeros_like(acc_ref)
    for half_ref, start in zip(half_refs, starts):
        q = half_ref[:, start : start + span]
        for r in range(0, rows, chunk):
            d = jnp.dot(unit_ref[r : r + chunk, :], q, preferred_element_type=F32)
            x = jnp.exp2(d * (LOG2E / STUDENT_TEMP))
            grad_ref[r : r + chunk, :] += lax.dot_general(x.astype(BF16), q, NT, preferred_element_type=F32)
            acc_ref[r : r + chunk, :] += lane_groups(x)


def gather_body(width, chunk, size, *refs):
    e_refs, (inv_ref, row_ref, p_ref, scale_ref) = refs[:PARTS], refs[PARTS : PARTS + 4]
    stay_ref, leave_ref, b_ref, flat_ref, held, sem = refs[PARTS + 4 :]
    rows, span = e_refs[0].shape
    unfold(inv_ref[...], flat_ref)
    b_ref[...] = jnp.zeros_like(b_ref)

    def step(start, e_ref, i, slot):
        here = aligned(i * width, width)
        cols = aligned(start + i * width, width)
        half = (held[slot].astype(F32) * scale_ref[:, cols]).astype(BF16)
        q = (half.astype(F32) * flat_ref[:, cols]).astype(BF16)
        for r in range(0, rows, chunk):
            b_ref[r : r + chunk, :] += lax.dot_general(e_ref[r : r + chunk, here], q, NT, preferred_element_type=F32)

    works = [functools.partial(step, k * span, e_ref) for k, e_ref in enumerate(e_refs)]
    stream([p_ref.at[:, k * span : (k + 1) * span] for k in range(PARTS)], held, sem, width, works)
    blocks_out(b_ref, 0, row_ref, 0, size, stay_ref)
    blocks_out(b_ref, rows // 2, row_ref, rows // 2, size, leave_ref)


def blocks_out(values_ref, start, row_ref, first, size, out_ref):
    for j in range(out_ref.shape[0]):
        out_ref[j, 0:size, :] = values_ref[start + j * size : start + (j + 1) * size, :]
        out_ref[j, size:, :] = jnp.zeros((8, out_ref.shape[2]), F32)
        s, lane = divmod(first + j * size, 128)
        out_ref[j, size : size + 1, 0:size] = row_ref[s : s + 1, lane : lane + size]


def pack_body(size, grad_ref, sum_ref, stay_ref, leave_ref, s_ref):
    rows_out(sum_ref, s_ref)
    middle = grad_ref.shape[0] // 2
    blocks_out(grad_ref, 0, s_ref, 0, size, stay_ref)
    blocks_out(grad_ref, middle, s_ref, middle, size, leave_ref)


def final_body(count, student_ref, *refs):
    (grads_ref, loss_ref) = refs[-2:]
    size, depth = student_ref.shape

    def total_of(parts):
        total = parts[0][...]
        for part in parts[1:]:
            total = total + part[...]
        line = total[size : size + 1, 0:size]
        return total[0:size, :] / wide(as_column(line), depth), line

    a, s_row = total_of(refs[:count])
    b, _ = total_of(refs[count:-2])
    floats, norm = norms_of(student_ref[...])
    unit = floats / norm
    direction = (a - b) / STUDENT_TEMP
    radial = jnp.sum(unit * direction, axis=1, keepdims=True)
    grads_ref[...] = (direction - unit * radial) / norm
    product = unit.astype(BF16).astype(F32) * b
    cross = jnp.sum(product, axis=1, keepdims=True) / STUDENT_TEMP
    cross = jnp.broadcast_to(cross, (size, 128))
    if size < 128:
        cross = jnp.concatenate([cross, jnp.zeros((128 - size, 128), F32)], axis=0)
    loss_ref[...] = jnp.log(s_row) - jnp.transpose(cross)[0:1, 0:size]


def on_device(row_devices, proto_devices, teacher_rows, student_rows, prototypes):
    size, depth = teacher_rows.shape
    cols = prototypes.shape[1]
    rows = size * proto_devices
    chips = range(2, proto_devices, 2)
    lines, blocks = rows // 128, cols // 128
    vm = pltpu.VMEM

    def swap(values, mask, axis="protos", count=proto_devices):
        return lax.ppermute(values, axis, [(i, i ^ mask) for i in range(count)])

    def over_rows(values):
        mask = 1
        while True:
            other = swap(values, mask, "rows", row_devices)
            mask *= 2
            if mask >= row_devices:
                return values, other
            values = values + other

    both = jnp.concatenate([teacher_rows, student_rows], axis=0)
    even = [both] + [swap(both, mask) for mask in chips]
    odd = [swap(part, 1) for part in even]

    width = min(2048, cols // PARTS)
    *made, col, unit, scale = call(
        functools.partial(exp_body, width, 256, proto_devices),
        [vm((rows, cols // PARTS), BF16)] * PARTS
        + [vm((depth, cols // PARTS), BF16)]
        + [pltpu.HBM((depth, cols // BLOCKS), BF16)] * (BLOCKS - KEPT)
        + [vm((blocks, 128), F32), vm((rows, depth), BF16), vm((1, cols), F32)],
        even + odd + [prototypes],
        [
            pltpu.VMEM((rows, depth), BF16),
            pltpu.VMEM((rows, 128), F32),
            pltpu.VMEM((1, cols), F32),
            pltpu.VMEM((2, depth, width), BF16),
            pltpu.SemaphoreType.DMA((2,)),
            pltpu.VMEM((cols // PARTS // width, depth, width), BF16),
            pltpu.SemaphoreType.DMA((cols // PARTS // width, width * BLOCKS // cols)),
        ],
        vmem=11,
        streamed=(proto_devices,),
        streamed_out=range(PARTS + 1, PARTS + 1 + BLOCKS - KEPT),
    )
    exps, kept, halves = made[:PARTS], made[PARTS], made[PARTS + 1 :]
    span = cols // BLOCKS
    halves = [(kept, k * span) for k in range(KEPT)] + [(half, 0) for half in halves]

    def student(blocks, held):
        arrays, starts = zip(*blocks)
        count = len(blocks)
        return call(
            functools.partial(student_body, 256, not held, span, starts),
            [vm((rows, depth), F32), vm((rows, 128), F32)],
            [unit, *arrays, *held],
            vmem=6,
            flops=4 * rows * depth * count * span,
            aliases={1 + count: 0, 2 + count: 1} if held else {},
        )

    held, taken = [], 0
    for count in PIECES:
        held = student(halves[taken : taken + count], held)
        taken += count

    for sweep in range(3):
        one, two = over_rows(col)
        inv, row, swapped = call(
            functools.partial(rowsum_body, width, 1024, 128),
            [vm((blocks, 128), F32), vm((lines, 128), F32), vm((lines, 128), F32)],
            [*exps, one, two],
            [pltpu.VMEM((rows, 128), F32), pltpu.VMEM((1, cols), F32)],
        )
        if sweep == 2:
            break
        row = row + swap(swapped, 1)
        col = call(
            functools.partial(colsum_body, cols // PARTS, size, PARTS),
            vm((blocks, 128), F32),
            [*exps, row] + [swap(row, mask) for mask in chips],
            [pltpu.VMEM((16, rows), BF16), pltpu.VMEM((1, cols), F32)],
        )

    def reduced(stay, leave):
        sums = stay + swap(leave, 1)
        return [sums[0]] + [swap(sums[mask // 2], mask) for mask in chips]

    block = vm((proto_devices // 2, size + 8, depth), F32)
    a_sums = reduced(*call(functools.partial(pack_body, size), [block, block], held, [pltpu.VMEM((lines, 128), F32)]))

    stay, leave = call(
        functools.partial(gather_body, width, 256, size),
        [block, block],
        [*exps, inv, row, prototypes, scale],
        [
            pltpu.VMEM((rows, depth), F32),
            pltpu.VMEM((1, cols), F32),
            pltpu.VMEM((2, depth, width), BF16),
            pltpu.SemaphoreType.DMA((2,)),
        ],
        vmem=6,
        flops=2 * rows * cols * depth,
        streamed=(PARTS + 2,),
    )
    b_sums = reduced(stay, leave)
    grads, loss = call(
        functools.partial(final_body, proto_devices // 2),
        [jax.ShapeDtypeStruct((size, depth), F32), jax.ShapeDtypeStruct((1, size), F32)],
        [student_rows] + a_sums + b_sums,
    )
    return grads, loss.reshape(size)


def solution(mesh):
    in_specs = (P(("rows", "protos"), None), P(("rows", "protos"), None), P(None, "protos"))
    out_specs = (P(("rows", "protos"), None), P(("rows", "protos")))
    return jax.shard_map(
        functools.partial(on_device, mesh.shape["rows"], mesh.shape["protos"]),
        mesh=mesh,
        in_specs=in_specs,
        out_specs=out_specs,
        check_vma=False,
    )
```

```python
import functools
import math

import jax
import jax.numpy as jnp
from jax import lax
from jax.experimental import pallas as pl
from jax.experimental.pallas import tpu as pltpu
from jax.sharding import PartitionSpec as P

EPSILON = 1e-06
TEACHER_TEMP = 0.04
STUDENT_TEMP = 0.1
LOG2E = math.log2(math.e)
F32 = jnp.float32
BF16 = jnp.bfloat16
MIB = 1 << 20
NT = (((1,), (1,)), ((), ()))
VMEM = pl.BlockSpec(memory_space=pltpu.VMEM)
HBM = pl.BlockSpec(memory_space=pltpu.HBM)
BLOCKS = 16
PIECES = (2, 2, 1, 2, 2, 2, 1, 1, 2, 1)
PARTS = 4
KEPT = BLOCKS // PARTS


def call(body, outs, args, scratch=(), vmem=4, flops=0, aliases={}, streamed=(), streamed_out=()):
    many = isinstance(outs, list)
    places = [HBM if i in streamed else VMEM for i in range(len(args))]
    made = pl.pallas_call(
        body,
        out_shape=outs,
        in_specs=places,
        out_specs=[HBM if i in streamed_out else VMEM for i in range(len(outs))] if many else VMEM,
        scratch_shapes=list(scratch),
        input_output_aliases=aliases,
        compiler_params=pltpu.CompilerParams(vmem_limit_bytes=vmem * MIB),
        cost_estimate=pl.CostEstimate(flops=flops, bytes_accessed=0, transcendentals=0),
    )
    spaces = [pltpu.HBM if i in streamed else pltpu.VMEM for i in range(len(args))]
    return made(*map(pltpu.with_memory_space_constraint, args, spaces))


def aligned(index, size):
    return pl.ds(pl.multiple_of(index, size), size)


def norms_of(rows):
    floats = rows.astype(F32)
    return floats, jnp.sqrt(jnp.sum(floats * floats, axis=1, keepdims=True) + EPSILON)


def as_column(row):
    size = row.shape[1]
    if size < 128:
        row = jnp.concatenate([row, jnp.zeros((1, 128 - size), F32)], axis=1)
    return jnp.transpose(jnp.broadcast_to(row, (128, 128)))[:size]


def lane_groups(values):
    parts = [values[:, s : s + 128] for s in range(0, values.shape[1], 128)]
    while len(parts) > 1:
        rest = parts[len(parts) // 2 * 2 :]
        parts = [a + b for a, b in zip(parts[::2], parts[1::2])] + rest
    return parts[0]


def wide(column, width):
    return jnp.concatenate([column] * (width // 128), axis=1)


def fold(flat_ref, out_ref):
    for s in range(out_ref.shape[0]):
        out_ref[s : s + 1, :] = flat_ref[:, s * 128 : (s + 1) * 128]


def unfold(values, flat_ref):
    for s in range(values.shape[0]):
        flat_ref[:, s * 128 : (s + 1) * 128] = values[s : s + 1, :]


def rows_out(acc_ref, row_ref):
    for s in range(row_ref.shape[0]):
        block = jnp.transpose(acc_ref[s * 128 : (s + 1) * 128, :])
        row_ref[s : s + 1, :] = jnp.sum(block, axis=0, keepdims=True)


def stream(source_refs, held_ref, sem_ref, width, work, before=None):
    steps = source_refs[0].shape[1] // width

    def copy(source_ref, i, slot):
        return pltpu.make_async_copy(source_ref.at[:, aligned(i * width, width)], held_ref.at[slot], sem_ref.at[slot])

    copy(source_refs[0], 0, 0).start()
    if before is not None:
        before()
    for k, source_ref in enumerate(source_refs):

        def step(i, _, k=k, source_ref=source_ref):
            slot, other = lax.rem(k * steps + i, 2), lax.rem(k * steps + i + 1, 2)

            @pl.when(i + 1 < steps)
            def _():
                copy(source_ref, i + 1, other).start()

            if k + 1 < len(source_refs):

                @pl.when(i + 1 == steps)
                def _():
                    copy(source_refs[k + 1], 0, other).start()

            copy(source_ref, i, slot).wait()
            work[k](i, slot)
            return 0

        lax.fori_loop(0, steps, step, 0)


def join_body(one_ref, two_ref, out_ref, sem_ref):
    size = one_ref.shape[0]
    copies = [
        pltpu.make_async_copy(one_ref, out_ref.at[0:size], sem_ref.at[0]),
        pltpu.make_async_copy(two_ref, out_ref.at[size:], sem_ref.at[1]),
    ]
    for copy in copies:
        copy.start()
    for copy in copies:
        copy.wait()


def exp_body(width, chunk, slots, *refs):
    parts, p_ref, refs = refs[:slots], refs[slots], refs[slots + 1 :]
    e_refs, kept_ref, half_refs, refs = refs[:PARTS], refs[PARTS], refs[PARTS + 1 :][: BLOCKS - KEPT], refs[PARTS + 1 + BLOCKS - KEPT :]
    col_ref, unit_ref, scale_ref, t_ref, a_ref, flat_ref, p_held, p_sem, out, out_sem = refs
    rows, span = e_refs[0].shape
    size = rows // slots

    def before():
        for m, part in enumerate(parts):
            here = slice(m * size, (m + 1) * size)
            teacher = part[0:size, :]
            t_ref[here, :] = teacher
            a_ref[here, :] = jnp.broadcast_to((LOG2E / TEACHER_TEMP) / norms_of(teacher)[1], (size, 128))
            floats, norm = norms_of(part[size:, :])
            unit_ref[here, :] = (floats / norm).astype(BF16)

    steps, block = span // width, half_refs[0].shape[1]

    def copies(at):
        slot, count = at % steps, width // block
        return [
            pltpu.make_async_copy(
                out.at[slot, :, q * block : (q + 1) * block], half_refs[at * count + q], out_sem.at[slot, q]
            )
            for q in range(count)
        ]

    def step(k, e_ref, i, slot):
        first = k * span
        if 0 < k < PARTS - 1:
            for q in range(steps):

                @pl.when(i == q)
                def _(q=q):
                    for copy in copies((k - 1) * steps + q):
                        copy.wait()

        for n in range(width // 256):
            here = aligned(i * width + n * 256, 256)
            cols = aligned(first + i * width + n * 256, 256)
            p = p_held[slot, :, n * 256 : (n + 1) * 256]
            floats = p.astype(F32)
            scale = lax.rsqrt(jnp.sum(floats * floats, axis=0, keepdims=True) + EPSILON)
            half = (floats * scale).astype(BF16)
            if k < PARTS - 1:
                out[i, :, n * 256 : (n + 1) * 256] = half
            else:
                kept_ref[:, here] = half
            scale_ref[:, cols] = scale
        for n in range(width // 256):
            here = aligned(i * width + n * 256, 256)
            cols = aligned(first + i * width + n * 256, 256)
            p = p_held[slot, :, n * 256 : (n + 1) * 256]
            scale = scale_ref[:, cols]
            acc = jnp.zeros((8, 256), F32)
            for r in range(0, rows, chunk):
                d = jnp.dot(t_ref[r : r + chunk, :], p, preferred_element_type=F32)
                e = jnp.exp2(d * wide(a_ref[r : r + chunk, :], 256) * scale)
                e_ref[r : r + chunk, here] = e.astype(BF16)
                acc = acc + jnp.sum(e.reshape(chunk // 8, 8, 256), axis=0)
            flat_ref[:, cols] = jnp.sum(acc, axis=0, keepdims=True)
        for q in range(steps if k < PARTS - 1 else 0):

            @pl.when(i == q)
            def _(q=q):
                for copy in copies(k * steps + q):
                    copy.start()

    works = [functools.partial(step, k, e_ref) for k, e_ref in enumerate(e_refs)]
    stream([p_ref.at[:, k * span : (k + 1) * span] for k in range(PARTS)], p_held, p_sem, width, works, before)
    fold(flat_ref, col_ref)
    for q in range(steps):
        for copy in copies((PARTS - 2) * steps + q):
            copy.wait()


def rowsum_body(width, group, chunk, *refs):
    e_refs, (one_ref, two_ref, inv_ref, row_ref, swap_ref, acc_ref, flat_ref) = refs[:-7], refs[-7:]
    rows, span = e_refs[0].shape
    inv = 1.0 / (one_ref[...] + two_ref[...])
    inv_ref[...] = inv
    unfold(inv, flat_ref)
    acc_ref[...] = jnp.zeros_like(acc_ref)

    def step(first, e_ref, i, _):
        for r in range(0, rows, chunk):
            acc = acc_ref[r : r + chunk, :]
            for n in range(width // group):
                here = aligned(i * width + n * group, group)
                cols = aligned(first + i * width + n * group, group)
                acc = acc + lane_groups(e_ref[r : r + chunk, here].astype(F32) * flat_ref[:, cols])
            acc_ref[r : r + chunk, :] = acc
        return 0

    for k, e_ref in enumerate(e_refs):
        lax.fori_loop(0, span // width, functools.partial(step, k * span, e_ref), 0)
    rows_out(acc_ref, row_ref)
    middle = row_ref.shape[0] // 2
    swap_ref[0:middle, :] = row_ref[middle:, :]
    swap_ref[middle:, :] = row_ref[0:middle, :]


def colsum_body(width, size, count, *refs):
    e_refs, parts, (col_ref, w_ref, flat_ref) = refs[:count], refs[count:-3], refs[-3:]
    rows, span = e_refs[0].shape
    for s in range(rows // 128):
        total = parts[0][s : s + 1, :]
        for j, part in enumerate(parts[1:], 1):
            line, lane = divmod(j * size, 128)
            other = part[s ^ line : (s ^ line) + 1, :]
            if lane:
                other = jnp.concatenate([other[:, lane:], other[:, :lane]], axis=1)
            total = total + other
        w = 1.0 / total
        high = w.astype(BF16).astype(F32)
        low = w - high
        both = jnp.concatenate([high, low, jnp.zeros((14, 128), F32)], axis=0)
        w_ref[:, s * 128 : (s + 1) * 128] = both.astype(BF16)

    def step(first, e_ref, i, _):
        sums = jnp.dot(w_ref[...], e_ref[:, aligned(i * width, width)], preferred_element_type=F32)
        flat_ref[:, aligned(first + i * width, width)] = sums[0:1, :] + sums[1:2, :]
        return 0

    for k, e_ref in enumerate(e_refs):
        lax.fori_loop(0, span // width, functools.partial(step, k * span, e_ref), 0)
    fold(flat_ref, col_ref)


def student_body(chunk, fresh, span, starts, unit_ref, *refs):
    half_refs, (grad_ref, acc_ref) = refs[: len(starts)], refs[-2:]
    rows = unit_ref.shape[0]
    if fresh:
        grad_ref[...] = jnp.zeros_like(grad_ref)
        acc_ref[...] = jnp.zeros_like(acc_ref)
    for half_ref, start in zip(half_refs, starts):
        q = half_ref[:, start : start + span]
        for r in range(0, rows, chunk):
            d = jnp.dot(unit_ref[r : r + chunk, :], q, preferred_element_type=F32)
            x = jnp.exp2(d * (LOG2E / STUDENT_TEMP))
            grad_ref[r : r + chunk, :] += lax.dot_general(x.astype(BF16), q, NT, preferred_element_type=F32)
            acc_ref[r : r + chunk, :] += lane_groups(x)


def gather_body(width, chunk, size, *refs):
    e_refs, (inv_ref, row_ref, p_ref, scale_ref) = refs[:PARTS], refs[PARTS : PARTS + 4]
    stay_ref, leave_ref, b_ref, flat_ref, held, sem = refs[PARTS + 4 :]
    rows, span = e_refs[0].shape

    def before():
        unfold(inv_ref[...], flat_ref)
        b_ref[...] = jnp.zeros_like(b_ref)

    def step(start, e_ref, i, slot):
        here = aligned(i * width, width)
        cols = aligned(start + i * width, width)
        half = (held[slot].astype(F32) * scale_ref[:, cols]).astype(BF16)
        q = (half.astype(F32) * flat_ref[:, cols]).astype(BF16)
        for r in range(0, rows, chunk):
            b_ref[r : r + chunk, :] += lax.dot_general(e_ref[r : r + chunk, here], q, NT, preferred_element_type=F32)

    works = [functools.partial(step, k * span, e_ref) for k, e_ref in enumerate(e_refs)]
    stream([p_ref.at[:, k * span : (k + 1) * span] for k in range(PARTS)], held, sem, width, works, before)
    blocks_out(b_ref, 0, row_ref, 0, size, stay_ref)
    blocks_out(b_ref, rows // 2, row_ref, rows // 2, size, leave_ref)


def blocks_out(values_ref, start, row_ref, first, size, out_ref):
    for j in range(out_ref.shape[0]):
        out_ref[j, 0:size, :] = values_ref[start + j * size : start + (j + 1) * size, :]
        out_ref[j, size:, :] = jnp.zeros((8, out_ref.shape[2]), F32)
        s, lane = divmod(first + j * size, 128)
        out_ref[j, size : size + 1, 0:size] = row_ref[s : s + 1, lane : lane + size]


def pack_body(size, grad_ref, sum_ref, stay_ref, leave_ref, s_ref):
    rows_out(sum_ref, s_ref)
    middle = grad_ref.shape[0] // 2
    blocks_out(grad_ref, 0, s_ref, 0, size, stay_ref)
    blocks_out(grad_ref, middle, s_ref, middle, size, leave_ref)


def final_body(count, student_ref, *refs):
    (grads_ref, loss_ref) = refs[-2:]
    size, depth = student_ref.shape

    def total_of(parts):
        total = parts[0][...]
        for part in parts[1:]:
            total = total + part[...]
        line = total[size : size + 1, 0:size]
        return total[0:size, :] / wide(as_column(line), depth), line

    a, s_row = total_of(refs[:count])
    b, _ = total_of(refs[count:-2])
    floats, norm = norms_of(student_ref[...])
    unit = floats / norm
    direction = (a - b) / STUDENT_TEMP
    radial = jnp.sum(unit * direction, axis=1, keepdims=True)
    grads_ref[...] = (direction - unit * radial) / norm
    product = unit.astype(BF16).astype(F32) * b
    cross = jnp.sum(product, axis=1, keepdims=True) / STUDENT_TEMP
    cross = jnp.broadcast_to(cross, (size, 128))
    if size < 128:
        cross = jnp.concatenate([cross, jnp.zeros((128 - size, 128), F32)], axis=0)
    loss_ref[...] = jnp.log(s_row) - jnp.transpose(cross)[0:1, 0:size]


def on_device(row_devices, proto_devices, teacher_rows, student_rows, prototypes):
    size, depth = teacher_rows.shape
    cols = prototypes.shape[1]
    rows = size * proto_devices
    chips = range(2, proto_devices, 2)
    lines, blocks = rows // 128, cols // 128
    vm = pltpu.VMEM

    def swap(values, mask, axis="protos", count=proto_devices):
        return lax.ppermute(values, axis, [(i, i ^ mask) for i in range(count)])

    def over_rows(values):
        mask = 1
        while True:
            other = swap(values, mask, "rows", row_devices)
            mask *= 2
            if mask >= row_devices:
                return values, other
            values = values + other

    both = call(
        join_body,
        vm((2 * size, depth), BF16),
        [teacher_rows, student_rows],
        [pltpu.SemaphoreType.DMA((2,))],
        streamed=(0, 1),
    )
    even = [both] + [swap(both, mask) for mask in chips]
    odd = [swap(part, 1) for part in even]

    width = min(2048, cols // PARTS)
    *made, col, unit, scale = call(
        functools.partial(exp_body, width, 256, proto_devices),
        [vm((rows, cols // PARTS), BF16)] * PARTS
        + [vm((depth, cols // PARTS), BF16)]
        + [pltpu.HBM((depth, cols // BLOCKS), BF16)] * (BLOCKS - KEPT)
        + [vm((blocks, 128), F32), vm((rows, depth), BF16), vm((1, cols), F32)],
        even + odd + [prototypes],
        [
            pltpu.VMEM((rows, depth), BF16),
            pltpu.VMEM((rows, 128), F32),
            pltpu.VMEM((1, cols), F32),
            pltpu.VMEM((2, depth, width), BF16),
            pltpu.SemaphoreType.DMA((2,)),
            pltpu.VMEM((cols // PARTS // width, depth, width), BF16),
            pltpu.SemaphoreType.DMA((cols // PARTS // width, width * BLOCKS // cols)),
        ],
        vmem=11,
        streamed=(proto_devices,),
        streamed_out=range(PARTS + 1, PARTS + 1 + BLOCKS - KEPT),
    )
    exps, kept, halves = made[:PARTS], made[PARTS], made[PARTS + 1 :]
    span = cols // BLOCKS
    halves = [(kept, k * span) for k in range(KEPT)] + [(half, 0) for half in halves]

    def student(blocks, held):
        arrays, starts = zip(*blocks)
        count = len(blocks)
        return call(
            functools.partial(student_body, 256, not held, span, starts),
            [vm((rows, depth), F32), vm((rows, 128), F32)],
            [unit, *arrays, *held],
            vmem=6,
            flops=4 * rows * depth * count * span,
            aliases={1 + count: 0, 2 + count: 1} if held else {},
        )

    held, taken = [], 0
    for count in PIECES:
        held = student(halves[taken : taken + count], held)
        taken += count

    for sweep in range(3):
        one, two = over_rows(col)
        inv, row, swapped = call(
            functools.partial(rowsum_body, width, 1024, 128),
            [vm((blocks, 128), F32), vm((lines, 128), F32), vm((lines, 128), F32)],
            [*exps, one, two],
            [pltpu.VMEM((rows, 128), F32), pltpu.VMEM((1, cols), F32)],
        )
        if sweep == 2:
            break
        row = row + swap(swapped, 1)
        col = call(
            functools.partial(colsum_body, cols // PARTS, size, PARTS),
            vm((blocks, 128), F32),
            [*exps, row] + [swap(row, mask) for mask in chips],
            [pltpu.VMEM((16, rows), BF16), pltpu.VMEM((1, cols), F32)],
        )

    def reduced(stay, leave):
        sums = stay + swap(leave, 1)
        return [sums[0]] + [swap(sums[mask // 2], mask) for mask in chips]

    block = vm((proto_devices // 2, size + 8, depth), F32)
    a_sums = reduced(*call(functools.partial(pack_body, size), [block, block], held, [pltpu.VMEM((lines, 128), F32)]))

    stay, leave = call(
        functools.partial(gather_body, 4096, 256, size),
        [block, block],
        [*exps, inv, row, prototypes, scale],
        [
            pltpu.VMEM((rows, depth), F32),
            pltpu.VMEM((1, cols), F32),
            pltpu.VMEM((2, depth, 4096), BF16),
            pltpu.SemaphoreType.DMA((2,)),
        ],
        vmem=10,
        flops=2 * rows * cols * depth,
        streamed=(PARTS + 2,),
    )
    b_sums = reduced(stay, leave)
    grads, loss = call(
        functools.partial(final_body, proto_devices // 2),
        [jax.ShapeDtypeStruct((size, depth), F32), jax.ShapeDtypeStruct((1, size), F32)],
        [student_rows] + a_sums + b_sums,
    )
    return grads, loss.reshape(size)


def solution(mesh):
    in_specs = (P(("rows", "protos"), None), P(("rows", "protos"), None), P(None, "protos"))
    out_specs = (P(("rows", "protos"), None), P(("rows", "protos")))
    return jax.shard_map(
        functools.partial(on_device, mesh.shape["rows"], mesh.shape["protos"]),
        mesh=mesh,
        in_specs=in_specs,
        out_specs=out_specs,
        check_vma=False,
    )
```

```python
import functools
import math

import jax
import jax.numpy as jnp
from jax import lax
from jax.experimental import pallas as pl
from jax.experimental.pallas import tpu as pltpu
from jax.sharding import PartitionSpec as P

EPSILON = 1e-06
TEACHER_TEMP = 0.04
STUDENT_TEMP = 0.1
LOG2E = math.log2(math.e)
F32 = jnp.float32
BF16 = jnp.bfloat16
MIB = 1 << 20
NT = (((1,), (1,)), ((), ()))
VMEM = pl.BlockSpec(memory_space=pltpu.VMEM)
HBM = pl.BlockSpec(memory_space=pltpu.HBM)
BLOCKS = 16
PIECES = (2, 2, 1, 2, 2, 2, 1, 1, 2, 1)
PARTS = 4
KEPT = BLOCKS // PARTS


def call(body, outs, args, scratch=(), vmem=4, flops=0, aliases={}, streamed=(), streamed_out=()):
    many = isinstance(outs, list)
    places = [HBM if i in streamed else VMEM for i in range(len(args))]
    made = pl.pallas_call(
        body,
        out_shape=outs,
        in_specs=places,
        out_specs=[HBM if i in streamed_out else VMEM for i in range(len(outs))] if many else VMEM,
        scratch_shapes=list(scratch),
        input_output_aliases=aliases,
        compiler_params=pltpu.CompilerParams(vmem_limit_bytes=vmem * MIB),
        cost_estimate=pl.CostEstimate(flops=flops, bytes_accessed=0, transcendentals=0),
    )
    spaces = [pltpu.HBM if i in streamed else pltpu.VMEM for i in range(len(args))]
    return made(*map(pltpu.with_memory_space_constraint, args, spaces))


def aligned(index, size):
    return pl.ds(pl.multiple_of(index, size), size)


def norms_of(rows):
    floats = rows.astype(F32)
    return floats, jnp.sqrt(jnp.sum(floats * floats, axis=1, keepdims=True) + EPSILON)


def as_column(row):
    size = row.shape[1]
    if size < 128:
        row = jnp.concatenate([row, jnp.zeros((1, 128 - size), F32)], axis=1)
    return jnp.transpose(jnp.broadcast_to(row, (128, 128)))[:size]


def lane_groups(values):
    parts = [values[:, s : s + 128] for s in range(0, values.shape[1], 128)]
    while len(parts) > 1:
        rest = parts[len(parts) // 2 * 2 :]
        parts = [a + b for a, b in zip(parts[::2], parts[1::2])] + rest
    return parts[0]


def wide(column, width):
    return jnp.concatenate([column] * (width // 128), axis=1)


def fold(flat_ref, out_ref):
    for s in range(out_ref.shape[0]):
        out_ref[s : s + 1, :] = flat_ref[:, s * 128 : (s + 1) * 128]


def unfold(values, flat_ref):
    for s in range(values.shape[0]):
        flat_ref[:, s * 128 : (s + 1) * 128] = values[s : s + 1, :]


def rows_out(acc_ref, row_ref):
    for s in range(row_ref.shape[0]):
        block = jnp.transpose(acc_ref[s * 128 : (s + 1) * 128, :])
        row_ref[s : s + 1, :] = jnp.sum(block, axis=0, keepdims=True)


def stream(source_refs, held_ref, sem_ref, width, work, before=None):
    steps = source_refs[0].shape[1] // width

    def copy(source_ref, i, slot):
        return pltpu.make_async_copy(source_ref.at[:, aligned(i * width, width)], held_ref.at[slot], sem_ref.at[slot])

    copy(source_refs[0], 0, 0).start()
    if before is not None:
        before()
    for k, source_ref in enumerate(source_refs):

        def step(i, _, k=k, source_ref=source_ref):
            slot, other = lax.rem(k * steps + i, 2), lax.rem(k * steps + i + 1, 2)

            @pl.when(i + 1 < steps)
            def _():
                copy(source_ref, i + 1, other).start()

            if k + 1 < len(source_refs):

                @pl.when(i + 1 == steps)
                def _():
                    copy(source_refs[k + 1], 0, other).start()

            copy(source_ref, i, slot).wait()
            work[k](i, slot)
            return 0

        lax.fori_loop(0, steps, step, 0)


def join_body(one_ref, two_ref, out_ref, sem_ref):
    size = one_ref.shape[0]
    copies = [
        pltpu.make_async_copy(one_ref, out_ref.at[0:size], sem_ref.at[0]),
        pltpu.make_async_copy(two_ref, out_ref.at[size:], sem_ref.at[1]),
    ]
    for copy in copies:
        copy.start()
    for copy in copies:
        copy.wait()


def exp_body(width, chunk, slots, *refs):
    parts, p_ref, refs = refs[:slots], refs[slots], refs[slots + 1 :]
    e_refs, kept_ref, half_refs, refs = refs[:PARTS], refs[PARTS], refs[PARTS + 1 :][: BLOCKS - KEPT], refs[PARTS + 1 + BLOCKS - KEPT :]
    col_ref, unit_ref, scale_ref, t_ref, a_ref, flat_ref, p_held, p_sem, out, out_sem = refs
    rows, span = e_refs[0].shape
    size = rows // slots

    def before():
        for m, part in enumerate(parts):
            here = slice(m * size, (m + 1) * size)
            teacher = part[0:size, :]
            t_ref[here, :] = teacher
            a_ref[here, :] = jnp.broadcast_to((LOG2E / TEACHER_TEMP) / norms_of(teacher)[1], (size, 128))
            floats, norm = norms_of(part[size:, :])
            unit_ref[here, :] = (floats / norm).astype(BF16)

    steps, block = span // width, half_refs[0].shape[1]

    def copies(at):
        slot, count = at % steps, width // block
        return [
            pltpu.make_async_copy(
                out.at[slot, :, q * block : (q + 1) * block], half_refs[at * count + q], out_sem.at[slot, q]
            )
            for q in range(count)
        ]

    def step(k, e_ref, i, slot):
        first = k * span
        if 0 < k < PARTS - 1:
            for q in range(steps):

                @pl.when(i == q)
                def _(q=q):
                    for copy in copies((k - 1) * steps + q):
                        copy.wait()

        for n in range(width // 256):
            here = aligned(i * width + n * 256, 256)
            cols = aligned(first + i * width + n * 256, 256)
            p = p_held[slot, :, n * 256 : (n + 1) * 256]
            floats = p.astype(F32)
            scale = lax.rsqrt(jnp.sum(floats * floats, axis=0, keepdims=True) + EPSILON)
            half = (floats * scale).astype(BF16)
            if k < PARTS - 1:
                out[i, :, n * 256 : (n + 1) * 256] = half
            else:
                kept_ref[:, here] = half
            scale_ref[:, cols] = scale
        for n in range(width // 256):
            here = aligned(i * width + n * 256, 256)
            cols = aligned(first + i * width + n * 256, 256)
            p = p_held[slot, :, n * 256 : (n + 1) * 256]
            scale = scale_ref[:, cols]
            acc = jnp.zeros((8, 256), F32)
            for r in range(0, rows, chunk):
                d = jnp.dot(t_ref[r : r + chunk, :], p, preferred_element_type=F32)
                e = jnp.exp2(d * wide(a_ref[r : r + chunk, :], 256) * scale)
                e_ref[r : r + chunk, here] = e.astype(BF16)
                acc = acc + jnp.sum(e.reshape(chunk // 8, 8, 256), axis=0)
            flat_ref[:, cols] = jnp.sum(acc, axis=0, keepdims=True)
        for q in range(steps if k < PARTS - 1 else 0):

            @pl.when(i == q)
            def _(q=q):
                for copy in copies(k * steps + q):
                    copy.start()

    works = [functools.partial(step, k, e_ref) for k, e_ref in enumerate(e_refs)]
    stream([p_ref.at[:, k * span : (k + 1) * span] for k in range(PARTS)], p_held, p_sem, width, works, before)
    fold(flat_ref, col_ref)
    for q in range(steps):
        for copy in copies((PARTS - 2) * steps + q):
            copy.wait()


def rowsum_body(width, group, chunk, exact, *refs):
    e_refs, (one_ref, two_ref, inv_ref, row_ref, swap_ref, acc_ref, flat_ref, wide_ref) = refs[:-8], refs[-8:]
    rows, span = e_refs[0].shape
    inv = 1.0 / (one_ref[...] + two_ref[...])
    inv_ref[...] = inv
    unfold(inv, flat_ref)
    if not exact:
        wide_ref[...] = jnp.broadcast_to(flat_ref[...], wide_ref.shape).astype(BF16)
    acc_ref[...] = jnp.zeros_like(acc_ref)

    def step(first, e_ref, i, _):
        for r in range(0, rows, chunk):
            acc = acc_ref[r : r + chunk, :]
            for n in range(width // group):
                here = aligned(i * width + n * group, group)
                cols = aligned(first + i * width + n * group, group)
                e = e_ref[r : r + chunk, here]
                if exact:
                    terms = e.astype(F32) * flat_ref[:, cols]
                else:
                    terms = (e * wide_ref[:, cols][0:1]).astype(F32)
                acc = acc + lane_groups(terms)
            acc_ref[r : r + chunk, :] = acc
        return 0

    for k, e_ref in enumerate(e_refs):
        lax.fori_loop(0, span // width, functools.partial(step, k * span, e_ref), 0)
    rows_out(acc_ref, row_ref)
    middle = row_ref.shape[0] // 2
    swap_ref[0:middle, :] = row_ref[middle:, :]
    swap_ref[middle:, :] = row_ref[0:middle, :]


def colsum_body(width, size, count, *refs):
    e_refs, parts, (col_ref, w_ref, flat_ref) = refs[:count], refs[count:-3], refs[-3:]
    rows, span = e_refs[0].shape
    for s in range(rows // 128):
        total = parts[0][s : s + 1, :]
        for j, part in enumerate(parts[1:], 1):
            line, lane = divmod(j * size, 128)
            other = part[s ^ line : (s ^ line) + 1, :]
            if lane:
                other = jnp.concatenate([other[:, lane:], other[:, :lane]], axis=1)
            total = total + other
        w = 1.0 / total
        high = w.astype(BF16).astype(F32)
        low = w - high
        both = jnp.concatenate([high, low, jnp.zeros((14, 128), F32)], axis=0)
        w_ref[:, s * 128 : (s + 1) * 128] = both.astype(BF16)

    def step(first, e_ref, i, _):
        sums = jnp.dot(w_ref[...], e_ref[:, aligned(i * width, width)], preferred_element_type=F32)
        flat_ref[:, aligned(first + i * width, width)] = sums[0:1, :] + sums[1:2, :]
        return 0

    for k, e_ref in enumerate(e_refs):
        lax.fori_loop(0, span // width, functools.partial(step, k * span, e_ref), 0)
    fold(flat_ref, col_ref)


def student_body(chunk, fresh, span, starts, unit_ref, *refs):
    half_refs, (grad_ref, acc_ref) = refs[: len(starts)], refs[-2:]
    rows = unit_ref.shape[0]
    if fresh:
        grad_ref[...] = jnp.zeros_like(grad_ref)
        acc_ref[...] = jnp.zeros_like(acc_ref)
    for half_ref, start in zip(half_refs, starts):
        q = half_ref[:, start : start + span]
        for r in range(0, rows, chunk):
            d = jnp.dot(unit_ref[r : r + chunk, :], q, preferred_element_type=F32)
            x = jnp.exp2(d * (LOG2E / STUDENT_TEMP))
            grad_ref[r : r + chunk, :] += lax.dot_general(x.astype(BF16), q, NT, preferred_element_type=F32)
            acc_ref[r : r + chunk, :] += lane_groups(x)


def gather_body(width, chunk, size, *refs):
    e_refs, (inv_ref, row_ref, p_ref, scale_ref) = refs[:PARTS], refs[PARTS : PARTS + 4]
    stay_ref, leave_ref, b_ref, flat_ref, held, sem = refs[PARTS + 4 :]
    rows, span = e_refs[0].shape

    def before():
        unfold(inv_ref[...], flat_ref)
        b_ref[...] = jnp.zeros_like(b_ref)

    def step(start, e_ref, i, slot):
        here = aligned(i * width, width)
        cols = aligned(start + i * width, width)
        half = (held[slot].astype(F32) * scale_ref[:, cols]).astype(BF16)
        q = (half.astype(F32) * flat_ref[:, cols]).astype(BF16)
        for r in range(0, rows, chunk):
            b_ref[r : r + chunk, :] += lax.dot_general(e_ref[r : r + chunk, here], q, NT, preferred_element_type=F32)

    works = [functools.partial(step, k * span, e_ref) for k, e_ref in enumerate(e_refs)]
    stream([p_ref.at[:, k * span : (k + 1) * span] for k in range(PARTS)], held, sem, width, works, before)
    blocks_out(b_ref, 0, row_ref, 0, size, stay_ref)
    blocks_out(b_ref, rows // 2, row_ref, rows // 2, size, leave_ref)


def blocks_out(values_ref, start, row_ref, first, size, out_ref):
    for j in range(out_ref.shape[0]):
        out_ref[j, 0:size, :] = values_ref[start + j * size : start + (j + 1) * size, :]
        out_ref[j, size:, :] = jnp.zeros((8, out_ref.shape[2]), F32)
        s, lane = divmod(first + j * size, 128)
        out_ref[j, size : size + 1, 0:size] = row_ref[s : s + 1, lane : lane + size]


def pack_body(size, grad_ref, sum_ref, stay_ref, leave_ref, s_ref):
    rows_out(sum_ref, s_ref)
    middle = grad_ref.shape[0] // 2
    blocks_out(grad_ref, 0, s_ref, 0, size, stay_ref)
    blocks_out(grad_ref, middle, s_ref, middle, size, leave_ref)


def final_body(count, student_ref, *refs):
    (grads_ref, loss_ref) = refs[-2:]
    size, depth = student_ref.shape

    def total_of(parts):
        total = parts[0][...]
        for part in parts[1:]:
            total = total + part[...]
        line = total[size : size + 1, 0:size]
        return total[0:size, :] / wide(as_column(line), depth), line

    a, s_row = total_of(refs[:count])
    b, _ = total_of(refs[count:-2])
    floats, norm = norms_of(student_ref[...])
    unit = floats / norm
    direction = (a - b) / STUDENT_TEMP
    radial = jnp.sum(unit * direction, axis=1, keepdims=True)
    grads_ref[...] = (direction - unit * radial) / norm
    product = unit.astype(BF16).astype(F32) * b
    cross = jnp.sum(product, axis=1, keepdims=True) / STUDENT_TEMP
    cross = jnp.broadcast_to(cross, (size, 128))
    if size < 128:
        cross = jnp.concatenate([cross, jnp.zeros((128 - size, 128), F32)], axis=0)
    loss_ref[...] = jnp.log(s_row) - jnp.transpose(cross)[0:1, 0:size]


def on_device(row_devices, proto_devices, teacher_rows, student_rows, prototypes):
    size, depth = teacher_rows.shape
    cols = prototypes.shape[1]
    rows = size * proto_devices
    chips = range(2, proto_devices, 2)
    lines, blocks = rows // 128, cols // 128
    vm = pltpu.VMEM

    def swap(values, mask, axis="protos", count=proto_devices):
        return lax.ppermute(values, axis, [(i, i ^ mask) for i in range(count)])

    def over_rows(values):
        mask = 1
        while True:
            other = swap(values, mask, "rows", row_devices)
            mask *= 2
            if mask >= row_devices:
                return values, other
            values = values + other

    both = call(
        join_body,
        vm((2 * size, depth), BF16),
        [teacher_rows, student_rows],
        [pltpu.SemaphoreType.DMA((2,))],
        streamed=(0, 1),
    )
    even = [both] + [swap(both, mask) for mask in chips]
    odd = [swap(part, 1) for part in even]

    width = min(2048, cols // PARTS)
    *made, col, unit, scale = call(
        functools.partial(exp_body, width, 256, proto_devices),
        [vm((rows, cols // PARTS), BF16)] * PARTS
        + [vm((depth, cols // PARTS), BF16)]
        + [pltpu.HBM((depth, cols // BLOCKS), BF16)] * (BLOCKS - KEPT)
        + [vm((blocks, 128), F32), vm((rows, depth), BF16), vm((1, cols), F32)],
        even + odd + [prototypes],
        [
            pltpu.VMEM((rows, depth), BF16),
            pltpu.VMEM((rows, 128), F32),
            pltpu.VMEM((1, cols), F32),
            pltpu.VMEM((2, depth, width), BF16),
            pltpu.SemaphoreType.DMA((2,)),
            pltpu.VMEM((cols // PARTS // width, depth, width), BF16),
            pltpu.SemaphoreType.DMA((cols // PARTS // width, width * BLOCKS // cols)),
        ],
        vmem=11,
        streamed=(proto_devices,),
        streamed_out=range(PARTS + 1, PARTS + 1 + BLOCKS - KEPT),
    )
    exps, kept, halves = made[:PARTS], made[PARTS], made[PARTS + 1 :]
    span = cols // BLOCKS
    halves = [(kept, k * span) for k in range(KEPT)] + [(half, 0) for half in halves]

    def student(blocks, held):
        arrays, starts = zip(*blocks)
        count = len(blocks)
        return call(
            functools.partial(student_body, 256, not held, span, starts),
            [vm((rows, depth), F32), vm((rows, 128), F32)],
            [unit, *arrays, *held],
            vmem=6,
            flops=4 * rows * depth * count * span,
            aliases={1 + count: 0, 2 + count: 1} if held else {},
        )

    held, taken = [], 0
    for count in PIECES:
        held = student(halves[taken : taken + count], held)
        taken += count

    for sweep in range(3):
        one, two = over_rows(col)
        inv, row, swapped = call(
            functools.partial(rowsum_body, width, 1024, 128, sweep == 2),
            [vm((blocks, 128), F32), vm((lines, 128), F32), vm((lines, 128), F32)],
            [*exps, one, two],
            [pltpu.VMEM((rows, 128), F32), pltpu.VMEM((1, cols), F32), pltpu.VMEM((16, cols), BF16)],
        )
        if sweep == 2:
            break
        row = row + swap(swapped, 1)
        col = call(
            functools.partial(colsum_body, cols // PARTS, size, PARTS),
            vm((blocks, 128), F32),
            [*exps, row] + [swap(row, mask) for mask in chips],
            [pltpu.VMEM((16, rows), BF16), pltpu.VMEM((1, cols), F32)],
        )

    def reduced(stay, leave):
        sums = stay + swap(leave, 1)
        return [sums[0]] + [swap(sums[mask // 2], mask) for mask in chips]

    block = vm((proto_devices // 2, size + 8, depth), F32)
    a_sums = reduced(*call(functools.partial(pack_body, size), [block, block], held, [pltpu.VMEM((lines, 128), F32)]))

    stay, leave = call(
        functools.partial(gather_body, 4096, 512, size),
        [block, block],
        [*exps, inv, row, prototypes, scale],
        [
            pltpu.VMEM((rows, depth), F32),
            pltpu.VMEM((1, cols), F32),
            pltpu.VMEM((2, depth, 4096), BF16),
            pltpu.SemaphoreType.DMA((2,)),
        ],
        vmem=10,
        flops=2 * rows * cols * depth,
        streamed=(PARTS + 2,),
    )
    b_sums = reduced(stay, leave)
    grads, loss = call(
        functools.partial(final_body, proto_devices // 2),
        [jax.ShapeDtypeStruct((size, depth), F32), jax.ShapeDtypeStruct((1, size), F32)],
        [student_rows] + a_sums + b_sums,
    )
    return grads, loss.reshape(size)


def solution(mesh):
    in_specs = (P(("rows", "protos"), None), P(("rows", "protos"), None), P(None, "protos"))
    out_specs = (P(("rows", "protos"), None), P(("rows", "protos")))
    return jax.shard_map(
        functools.partial(on_device, mesh.shape["rows"], mesh.shape["protos"]),
        mesh=mesh,
        in_specs=in_specs,
        out_specs=out_specs,
        check_vma=False,
    )
```
